32 devices in a mesh: dp: 4 (over y, x), expert: 8 (over z, core).
Axes of the slice: x: 2, y: 2, z: 4, core: 2. Of those that a mesh axis runs over, the one named last changes fastest.
Arguments:
- tokens: bfloat16 [6144, 2048], P(('dp', 'expert')), may hold values from -6 to 6
- modality: int32 [6144], P(('dp', 'expert')), may hold values from 0 to 1, as said below
- local_expert: int32 [6144], P(('dp', 'expert')), may hold values from 0 to 1, as said below
- combine_weight: float32 [6144], P(('dp', 'expert')), may hold values from 0.3 to 1
- norm_gain: float32 [2, 2048], replicated, may hold values from 0.1 to 1.9
- gate_weight: bfloat16 [2048, 16384], P('dp', 'expert'), may hold values from -0.125 to 0.125
- up_weight: bfloat16 [2048, 16384], P('dp', 'expert'), may hold values from -0.125 to 0.125
- down_weight: bfloat16 [16384, 2048], P('expert', 'dp'), may hold values from -0.09375 to 0.09375
Outputs:
- mixed: bfloat16 [6144, 2048], P(('dp', 'expert'))
The draws below stay inside these ranges and needn't reach their ends.
Inputs may be any that keep to these rules, and one draw needn't show every extreme that they name: Expert e = modality * 2 + local_expert. Among the 192 rows of each device (aligned blocks in order) no expert is chosen by more than 72 rows, and on every device one expert is chosen by exactly 72. `local_expert`: drawn together with modality under the bound stated there.
All inputs are finite; a program needn't handle non-finite values.
Results may differ from the reference program's by a relative error of at most 0.005.
Values may be sent and summed in bfloat16 or wider, within the bound.
A program may use at most 128 MiB of HBM per device.

```python
import jax
import jax.numpy as jnp
from jax import lax

D = 2048
H = 4096
EXP_MOD = 2
EXPERTS = 4
TOK_DEV = 192
CAP = 72
TOKENS = 6144
N_EXPERT = 8


def routing(key):
    blocks = TOKENS // TOK_DEV
    block_keys = jax.random.split(jax.random.fold_in(key, 7), blocks)

    def one_block(block_key):
        key_counts, key_order, key_rank = jax.random.split(block_key, 3)
        count_keys = jax.random.split(key_counts, EXPERTS)
        count_list = [jnp.int32(CAP)]
        remaining = jnp.int32(TOK_DEV - CAP)
        for step_index in range(EXPERTS - 2):
            slots_after = EXPERTS - 2 - step_index
            low_bound = jnp.maximum(1, remaining - slots_after * CAP)
            high_bound = jnp.minimum(CAP, remaining - slots_after)
            chosen = jax.random.randint(count_keys[step_index], (), low_bound, high_bound + 1, dtype=jnp.int32)
            count_list.append(chosen)
            remaining = remaining - chosen
        count_list.append(remaining)
        counts = jnp.stack(count_list).astype(jnp.int32)
        expert_order = jax.random.permutation(key_order, EXPERTS).astype(jnp.int32)
        bounds_cum = jnp.cumsum(counts)
        row_rank = jax.random.permutation(key_rank, TOK_DEV).astype(jnp.int32)
        slot_group = jnp.sum((row_rank[:, None] >= bounds_cum[None, :]).astype(jnp.int32), axis=1)
        return expert_order[slot_group]
    return jax.vmap(one_block)(block_keys).reshape(TOKENS).astype(jnp.int32)


def draw_modality(key, part):
    return (routing(key) // EXP_MOD).astype(jnp.int32)


def draw_local_expert(key, part):
    return (routing(key) % EXP_MOD).astype(jnp.int32)


def block_scale(own_key, shape, cuts, low, top_value):
    loudness = 1.0
    for axis_at, parts in cuts:
        draws = jax.random.uniform(jax.random.fold_in(jax.random.fold_in(own_key, 6), axis_at), (parts,), jnp.float32, low / len(cuts), top_value / len(cuts))
        loudness = loudness * jnp.repeat(jnp.exp(draws), shape[axis_at] // parts).reshape((-1,) + (1,) * (len(shape) - 1 - axis_at))
    return loudness


def gaussian(rng, shape, spread, reach, cuts=(), held_as=jnp.bfloat16):
    gain = block_scale(rng, shape, cuts, -0.22, 0.18) if cuts else 1.0
    drawn = jax.random.normal(rng, shape, jnp.float32) * spread * gain
    return jnp.minimum(jnp.maximum(drawn, -reach), reach).astype(held_as)


def setup_inputs(seed: int = 0) -> dict:
    streams_of = jax.random.split(jax.random.key(seed), 9)
    tokens = gaussian(streams_of[0], (TOKENS, D), 1.0, 6.0, ((0, 32),))
    modality = draw_modality(jax.random.fold_in(streams_of[8], 71), 0)
    local_expert = draw_local_expert(jax.random.fold_in(streams_of[8], 71), 0)
    combine_weight = jnp.clip(0.3 + 0.7 * jax.random.uniform(streams_of[3], (TOKENS,), jnp.float32) ** block_scale(streams_of[3], (TOKENS,), ((0, 32),), -0.2, 0.2), 0.3, 1.0)
    norm_gain = jnp.clip(1.0 + 0.18 * jax.random.normal(streams_of[4], (2, D), jnp.float32), 0.1, 1.9)
    gate_weight = gaussian(streams_of[5], (D, EXPERTS * H), D ** -0.5, 0.125, ((0, 4), (1, 8)))
    up_weight = gaussian(streams_of[6], (D, EXPERTS * H), D ** -0.5, 0.125, ((0, 4), (1, 8)))
    down_weight = gaussian(streams_of[7], (EXPERTS * H, D), H ** -0.5, 0.09375, ((0, 8), (1, 4)))
    return dict(tokens=tokens, modality=modality, local_expert=local_expert, combine_weight=combine_weight, norm_gain=norm_gain, gate_weight=gate_weight, up_weight=up_weight, down_weight=down_weight)


def reference(tokens, modality, local_expert, combine_weight, norm_gain, gate_weight, up_weight, down_weight):
    resid = tokens.astype(jnp.float32)
    root_mean = jnp.sqrt(lax.optimization_barrier(jnp.mean(resid * resid, axis=1, keepdims=True)) + 1e-05)
    row_gain = jnp.where(modality[:, None] == 0, norm_gain[0][None, :], norm_gain[1][None, :])
    normed = (resid / root_mean * row_gain).astype(jnp.bfloat16)
    route = modality * EXP_MOD + local_expert
    blocks = TOKENS // TOK_DEV
    routed = route.reshape(blocks, TOK_DEV)
    onehot = (routed[:, :, None] == jnp.arange(EXPERTS, dtype=jnp.int32)[None, None, :]).astype(jnp.int32)
    row_rank = lax.optimization_barrier(jnp.sum((jnp.cumsum(onehot, axis=1) - 1) * onehot, axis=2))
    block_ids = jnp.arange(blocks, dtype=jnp.int32)[:, None]
    slot_index = ((routed * blocks + block_ids) * CAP + row_rank).reshape(-1).astype(jnp.int32)
    token_ids = jnp.arange(TOKENS, dtype=jnp.int32)
    slot_table = jnp.full((EXPERTS * blocks * CAP,), TOKENS, dtype=jnp.int32).at[slot_index].set(token_ids)
    padded = jnp.concatenate([normed, jnp.zeros((1, D), jnp.bfloat16)], axis=0)
    gathered = padded[slot_table].reshape(EXPERTS, blocks * CAP, D)
    group = N_EXPERT // EXPERTS
    quarter = H // group

    def per_expert(expert_index):
        rows_e = lax.dynamic_index_in_dim(gathered, expert_index, 0, keepdims=False)
        total = jnp.zeros((blocks * CAP, D), jnp.float32)
        for part_index in range(group):
            first_col = (expert_index * H + part_index * quarter).astype(jnp.int32)
            gate_part = lax.dynamic_slice_in_dim(gate_weight, first_col, quarter, 1)
            up_part = lax.dynamic_slice_in_dim(up_weight, first_col, quarter, 1)
            down_part = lax.dynamic_slice_in_dim(down_weight, first_col, quarter, 0)
            gate_acts = jnp.dot(rows_e, gate_part, preferred_element_type=jnp.float32)
            up_acts = jnp.dot(rows_e, up_part, preferred_element_type=jnp.float32)
            hidden = (jax.nn.silu(gate_acts) * up_acts).astype(jnp.bfloat16)
            partial_out = jnp.dot(hidden, down_part, preferred_element_type=jnp.float32).astype(jnp.bfloat16)
            partial_out = lax.optimization_barrier(partial_out)
            total = total + partial_out.astype(jnp.float32)
        return total
    expert_sums = lax.map(per_expert, jnp.arange(EXPERTS, dtype=jnp.int32))
    moe_out = jnp.zeros((TOKENS + 1, D), jnp.float32).at[slot_table].add(expert_sums.reshape(-1, D))[:TOKENS]
    return (resid + combine_weight[:, None] * moe_out).astype(jnp.bfloat16)
```

```python
import functools

import jax
import jax.numpy as jnp
from jax import lax
from jax.experimental import pallas as pl
from jax.experimental.pallas import tpu as pltpu
from jax.sharding import PartitionSpec as P

EXP_MOD = 2
EXPERTS = 4
CAP = 72
SLOTS = -(-CAP // 16) * 16
ROWS = EXPERTS * CAP
VMEM_LIMIT = 60 << 20


def tiles(total, width, step):
    def one(i, carry):
        step(pl.multiple_of(i * width, width))
        return carry

    lax.fori_loop(0, total // width, one, 0)


def kernel(
    dp, share, group,
    buf, gate, up, down,
    out,
    zin, arr, wg, wu, wd, hid, part, core_in, dp_in, wide, zout,
    z_s, z_r, w_s, w_r, w_l, b_s, b_r, f_s, f_r, c_s, c_r, d_s, d_r, o_s, o_r, l_s,
):
    d = lax.axis_index("dp")
    p = lax.axis_index("expert")
    e, g = p // group, lax.rem(p, group)
    base, r = d // share * share, lax.rem(d, share)
    deep, cut, width = gate.shape[0], down.shape[1], buf.shape[-1]
    units = wg.shape[1]

    def dp_peer(k):
        return (lax.rem(d + k, dp), p)

    def share_peer(k):
        return (base + lax.rem(r + k, share), p)

    def z_peer(k):
        return (d, lax.rem(e + k, EXPERTS) * group + g)

    def core_peer(m):
        return (d, e * group + lax.rem(g + m, group))

    def send(src, dst, s, q, to):
        return pltpu.make_async_remote_copy(
            src_ref=src, dst_ref=dst, send_sem=s, recv_sem=q,
            device_id=to, device_id_type=pl.DeviceIdType.MESH,
        )

    peers = (
        [dp_peer(k) for k in range(1, dp)]
        + [z_peer(k) for k in range(1, EXPERTS)]
        + [core_peer(m) for m in range(1, group)]
    )
    barrier = pltpu.get_barrier_semaphore()
    for peer in peers:
        pl.semaphore_signal(barrier, inc=1, device_id=peer, device_id_type=pl.DeviceIdType.MESH)
    pl.semaphore_wait(barrier, len(peers))

    sent = []

    def go(copy):
        copy.start()
        sent.append(copy)
        return copy

    z_copies = [
        go(send(buf.at[k], zin.at[k], z_s.at[k], z_r.at[k], z_peer(k))) for k in range(1, EXPERTS)
    ]
    own_rows = pltpu.make_async_copy(buf.at[0], zin.at[0], l_s.at[0])
    own_rows.start()

    my_units = pl.ds(pl.multiple_of(r * units, units), units)
    my_deep = pl.ds(pl.multiple_of(d * deep, deep), deep)
    my_cut = pl.ds(pl.multiple_of(d * cut, cut), cut)
    own_w = [
        pltpu.make_async_copy(gate.at[:, my_units], wg.at[my_deep, :], w_l.at[0]),
        pltpu.make_async_copy(up.at[:, my_units], wu.at[my_deep, :], w_l.at[1]),
        pltpu.make_async_copy(down.at[my_units, :], wd.at[:, my_cut], w_l.at[2]),
    ]
    for copy in own_w:
        copy.start()

    def weight_copies(which):
        made = []
        for k in range(1, dp):
            theirs = lax.rem(lax.rem(d + k, dp), share)
            units_k = pl.ds(pl.multiple_of(theirs * units, units), units)
            if which == 2:
                src, dst = down.at[units_k, :], wd.at[:, my_cut]
            else:
                src, dst = (gate, up)[which].at[:, units_k], (wg, wu)[which].at[my_deep, :]
            made.append(go(send(src, dst, w_s.at[which, k], w_r.at[which, k], dp_peer(k))))
        return made

    gate_copies = weight_copies(0)
    up_copies = weight_copies(1)

    own_rows.wait()
    for copy in z_copies:
        copy.wait_recv()
    for i in range(EXPERTS):

        def widen(at, i=i):
            wide[i * CAP : (i + 1) * CAP, pl.ds(at, 256)] = zin[i, :, pl.ds(at, 256)].astype(
                jnp.float32
            )[:CAP]

        tiles(width, 256, widen)

    def narrow(at):
        arr[0, 0, :, pl.ds(at, 256)] = wide[:, pl.ds(at, 256)].astype(jnp.bfloat16)

    tiles(width, 256, narrow)

    rows_in = {}
    for k in range(1, share):
        rows_in[k] = go(send(arr.at[0, 0], arr.at[k, 0], b_s.at[k], b_r.at[k], share_peer(k)))
    core_rows = {}

    def forward(k):
        for m in range(1, group):
            core_rows[k, m] = go(
                send(arr.at[k, 0], arr.at[k, m], f_s.at[k, m], f_r.at[k, m], core_peer(m))
            )

    forward(0)
    down_copies = weight_copies(2)
    for k in range(1, share):
        rows_in[k].wait_recv()
        forward(k)

    for copy in (*own_w[:2],):
        copy.wait()
    for copy in (*gate_copies, *up_copies):
        copy.wait_recv()

    core_sums = {}
    dp_sums = {}
    rows = group * ROWS

    def finish(k):
        for m in range(1, group):
            core_sums[k, m].wait_recv()

        def add(at):
            cols = pl.ds(at, 256)
            total = part[k, 0, :, cols].astype(jnp.float32)
            for m in range(1, group):
                total = total + core_in[k, m, :, cols].astype(jnp.float32)
            part[k, 0, :, cols] = total.astype(jnp.bfloat16)

        tiles(width, 256, add)
        if k:
            dp_sums[k] = go(
                send(part.at[k, 0], dp_in.at[k], d_s.at[k], d_r.at[k], share_peer(share - k))
            )

    order = [*range(1, share), 0]
    for n, k in enumerate(order):
        for m in range(1, group):
            core_rows[k, m].wait_recv()

        def first(at, k=k):
            cols = pl.ds(at, 256)
            x = arr[k].reshape(rows, width)
            gated = jnp.dot(x, wg[:, cols], preferred_element_type=jnp.float32)
            lifted = jnp.dot(x, wu[:, cols], preferred_element_type=jnp.float32)
            hid[:, cols] = (gated / (1.0 + jnp.exp(-gated)) * lifted).astype(jnp.bfloat16)

        tiles(units, 256, first)
        if n == 0:
            own_w[2].wait()
            for copy in down_copies:
                copy.wait_recv()

        def second(at, k=k):
            cols = pl.ds(at, 256)
            made = jnp.dot(hid[...], wd[:, cols], preferred_element_type=jnp.float32)
            part[k, :, :, cols] = made.astype(jnp.bfloat16).reshape(group, ROWS, 256)

        tiles(width, 256, second)
        for m in range(1, group):
            core_sums[k, m] = go(
                send(part.at[k, m], core_in.at[k, m], c_s.at[k, m], c_r.at[k, m], core_peer(group - m))
            )
        if n:
            finish(order[n - 1])
    finish(order[-1])

    for k in range(1, share):
        dp_sums[k].wait_recv()

    def gather(at):
        cols = pl.ds(at, 256)
        total = part[0, 0, :, cols].astype(jnp.float32)
        for k in range(1, share):
            total = total + dp_in[k, :, cols].astype(jnp.float32)
        wide[:, cols] = total

    tiles(width, 256, gather)
    home = []
    for i in [*range(1, EXPERTS), 0]:
        to = out if i == 0 else zout

        def split(at, i=i, to=to):
            cols = pl.ds(at, 256)
            full = jnp.concatenate(
                [wide[i * CAP : (i + 1) * CAP, cols], jnp.zeros((SLOTS - CAP, 256), jnp.float32)], 0
            )
            to[i, :, cols] = full.astype(jnp.bfloat16)

        tiles(width, 256, split)
        if i:
            home.append(
                go(send(zout.at[i], out.at[i], o_s.at[i], o_r.at[i], z_peer(EXPERTS - i)))
            )
    for copy in home:
        copy.wait_recv()
    for copy in sent:
        copy.wait_send()


def shared_by(dp, group, width, hidden):
    for share in range(dp, 0, -1):
        if dp % share or hidden % share or hidden // share % 256:
            continue
        block = ROWS * width * 2
        units = hidden // share
        held = (
            block * (share * group * 2 + share * (group - 1) + share + 2)
            + 3 * width * units * 2
            + group * ROWS * units * 2
            + 4 * EXPERTS * SLOTS * width * 2
        )
        if held <= VMEM_LIMIT * 2 // 3:
            return share
    return 1


def experts(buffer, gate, up, down):
    dp, group = lax.axis_size("dp"), lax.axis_size("expert") // EXPERTS
    width, hidden = buffer.shape[-1], gate.shape[1]
    share = shared_by(dp, group, width, hidden)
    units = hidden // share
    bf16, dma = jnp.bfloat16, pltpu.SemaphoreType.DMA
    whole = pl.BlockSpec(memory_space=pltpu.VMEM)
    far = pl.BlockSpec(memory_space=pl.ANY)
    pairs = lambda *shape: [dma(shape), dma(shape)]
    return pl.pallas_call(
        functools.partial(kernel, dp, share, group),
        out_shape=jax.ShapeDtypeStruct(buffer.shape, bf16),
        in_specs=[whole, far, far, far],
        out_specs=whole,
        scratch_shapes=[
            pltpu.VMEM((EXPERTS, SLOTS, width), bf16),
            pltpu.VMEM((share, group, ROWS, width), bf16),
            pltpu.VMEM((width, units), bf16),
            pltpu.VMEM((width, units), bf16),
            pltpu.VMEM((units, width), bf16),
            pltpu.VMEM((group * ROWS, units), bf16),
            pltpu.VMEM((share, group, ROWS, width), bf16),
            pltpu.VMEM((share, group, ROWS, width), bf16),
            pltpu.VMEM((share, ROWS, width), bf16),
            pltpu.VMEM((ROWS, width), jnp.float32),
            pltpu.VMEM((EXPERTS, SLOTS, width), bf16),
            *pairs(EXPERTS),
            *pairs(3, dp),
            dma((3,)),
            *pairs(share),
            *pairs(share, group),
            *pairs(share, group),
            *pairs(share),
            *pairs(EXPERTS),
            dma((1,)),
        ],
        compiler_params=pltpu.CompilerParams(
            collective_id=0, has_side_effects=True, vmem_limit_bytes=VMEM_LIMIT
        ),
        cost_estimate=pl.CostEstimate(
            flops=6 * share * group * ROWS * width * units,
            bytes_accessed=3 * width * hidden * 2,
            transcendentals=share * group * ROWS * units,
        ),
    )(buffer, gate, up, down)


def body(
    tokens, modality, local_expert, combine_weight, norm_gain, gate_weight, up_weight, down_weight
):
    count, width = tokens.shape
    resid = tokens.astype(jnp.float32)
    root_mean = jnp.sqrt(jnp.mean(resid * resid, axis=1, keepdims=True) + 1e-05)
    row_gain = jnp.where(modality[:, None] == 0, norm_gain[0][None, :], norm_gain[1][None, :])
    normed = (resid / root_mean * row_gain).astype(jnp.bfloat16)
    route = modality * EXP_MOD + local_expert
    at = jnp.arange(count, dtype=jnp.int32)
    earlier = (route[:, None] == route[None, :]) & (at[None, :] < at[:, None])
    row_rank = jnp.sum(earlier.astype(jnp.int32), axis=1)
    own = lax.axis_index("expert") // (lax.axis_size("expert") // EXPERTS)
    position = (route - own + EXPERTS) % EXPERTS * SLOTS + row_rank
    placing = (
        position[:, None] == jnp.arange(EXPERTS * SLOTS, dtype=jnp.int32)[None, :]
    ).astype(jnp.bfloat16)
    buffer = jnp.einsum("ts,td->sd", placing, normed, preferred_element_type=jnp.float32)
    buffer = buffer.astype(jnp.bfloat16).reshape(EXPERTS, SLOTS, width)
    summed = experts(buffer, gate_weight, up_weight, down_weight)
    moe_out = jnp.dot(
        placing, summed.reshape(EXPERTS * SLOTS, width), preferred_element_type=jnp.float32
    )
    return (resid + combine_weight[:, None] * moe_out).astype(jnp.bfloat16)


def solution(mesh):
    in_specs = (
        P(("dp", "expert"), None),
        P(("dp", "expert")),
        P(("dp", "expert")),
        P(("dp", "expert")),
        P(),
        P("dp", "expert"),
        P("dp", "expert"),
        P("expert", "dp"),
    )
    out_specs = P(("dp", "expert"), None)
    return jax.shard_map(body, mesh=mesh, in_specs=in_specs, out_specs=out_specs, check_vma=False)
```

```python
import functools

import jax
import jax.numpy as jnp
from jax import lax
from jax.experimental import pallas as pl
from jax.experimental.pallas import tpu as pltpu
from jax.sharding import PartitionSpec as P

EXP_MOD = 2
EXPERTS = 4
CAP = 72
SLOTS = -(-CAP // 16) * 16
ROWS = EXPERTS * CAP
PIECES = 4
VMEM_LIMIT = 60 << 20


def partner(i, k, n):
    if n & (n - 1):
        return lax.rem(i + k, n)
    for bit in range(n.bit_length()):
        if k >> bit & 1:
            i = i + (1 - 2 * (i // (1 << bit) % 2)) * (1 << bit)
    return i


def back(k, n):
    return n - k if n & (n - 1) else k


def tiles(total, width, step):
    def one(i, carry):
        step(pl.multiple_of(i * width, width))
        return carry

    lax.fori_loop(0, total // width, one, 0)


def kernel(
    dp, share, group,
    buf, gate, up, down,
    out,
    zin, arr, wg, wu, wd, hid, part, core_in, dp_in, relay_in, wide, zout,
    z_s, z_r, w_s, w_r, w_l, b_s, b_r, f_s, f_r, c_s, c_r, d_s, d_r, r_s, r_r, o_s, o_r, l_s,
):
    d = lax.axis_index("dp")
    p = lax.axis_index("expert")
    e, g = p // group, lax.rem(p, group)
    base, r = d // share * share, lax.rem(d, share)
    deep, cut, width = gate.shape[0], down.shape[1], buf.shape[-1]
    units = wg.shape[1]
    half, piece = ROWS // 2, width // PIECES
    relay = share == 4
    low, high = pl.ds(0, half), pl.ds(half, half)

    def dp_peer(k):
        return (partner(d, k, dp), p)

    def share_peer(k):
        return (base + partner(r, k, share), p)

    def z_peer(k):
        return (d, lax.rem(e + k, EXPERTS) * group + g)

    def core_peer(m):
        return (d, e * group + lax.rem(g + m, group))

    def send(src, dst, s, q, to):
        return pltpu.make_async_remote_copy(
            src_ref=src, dst_ref=dst, send_sem=s, recv_sem=q,
            device_id=to, device_id_type=pl.DeviceIdType.MESH,
        )

    peers = (
        [dp_peer(k) for k in range(1, dp)]
        + [z_peer(k) for k in range(1, EXPERTS)]
        + [core_peer(m) for m in range(1, group)]
    )
    barrier = pltpu.get_barrier_semaphore()
    for peer in peers:
        pl.semaphore_signal(barrier, inc=1, device_id=peer, device_id_type=pl.DeviceIdType.MESH)
    pl.semaphore_wait(barrier, len(peers))

    sent = []

    def go(copy):
        copy.start()
        sent.append(copy)
        return copy

    z_copies = [
        go(send(buf.at[k], zin.at[k], z_s.at[k], z_r.at[k], z_peer(k))) for k in range(1, EXPERTS)
    ]
    own_rows = pltpu.make_async_copy(buf.at[0], zin.at[0], l_s.at[0])
    own_rows.start()

    my_units = pl.ds(pl.multiple_of(r * units, units), units)
    my_deep = pl.ds(pl.multiple_of(d * deep, deep), deep)
    my_cut = pl.ds(pl.multiple_of(d * cut, cut), cut)
    own_w = [
        pltpu.make_async_copy(gate.at[:, my_units], wg.at[my_deep, :], w_l.at[0]),
        pltpu.make_async_copy(up.at[:, my_units], wu.at[my_deep, :], w_l.at[1]),
        pltpu.make_async_copy(down.at[my_units, :], wd.at[:, my_cut], w_l.at[2]),
    ]
    for copy in own_w:
        copy.start()

    def weight_copies(which):
        made = []
        for k in range(1, dp):
            theirs = lax.rem(partner(d, k, dp), share)
            units_k = pl.ds(pl.multiple_of(theirs * units, units), units)
            if which == 2:
                src, dst = down.at[units_k, :], wd.at[:, my_cut]
            else:
                src, dst = (gate, up)[which].at[:, units_k], (wg, wu)[which].at[my_deep, :]
            made.append(go(send(src, dst, w_s.at[which, k], w_r.at[which, k], dp_peer(k))))
        return made

    gate_copies = weight_copies(0)
    up_copies = weight_copies(1)

    own_rows.wait()
    for copy in z_copies:
        copy.wait_recv()
    for i in range(EXPERTS):

        def widen(at, i=i):
            wide[i * CAP : (i + 1) * CAP, pl.ds(at, 256)] = zin[i, :, pl.ds(at, 256)].astype(
                jnp.float32
            )[:CAP]

        tiles(width, 256, widen)

    def narrow(at):
        arr[0, 0, :, pl.ds(at, 256)] = wide[:, pl.ds(at, 256)].astype(jnp.bfloat16)

    tiles(width, 256, narrow)

    rows_in = {}
    for k in range(1, share):
        if not (relay and k == 3):
            rows_in[k] = [
                go(send(arr.at[0, 0], arr.at[k, 0], b_s.at[k], b_r.at[k], share_peer(k)))
            ]
    core_rows = {}

    def forward(k):
        for m in range(1, group):
            core_rows[k, m] = go(
                send(arr.at[k, 0], arr.at[k, m], f_s.at[k, m], f_r.at[k, m], core_peer(m))
            )

    forward(0)
    down_copies = weight_copies(2)
    if relay:
        rows_in[3] = []
    for k in range(1, share):
        for copy in rows_in[k]:
            copy.wait_recv()
        if relay and k < 3:
            part_k = (low, high)[k - 1]
            rows_in[3].append(
                go(send(
                    arr.at[k, 0, part_k, :], arr.at[3, 0, part_k, :],
                    b_s.at[share + k], b_r.at[share + k], share_peer(3 - k),
                ))
            )
        forward(k)

    for copy in (*own_w[:2],):
        copy.wait()
    for copy in (*gate_copies, *up_copies):
        copy.wait_recv()

    core_sums = {}
    dp_sums = {}
    relayed = {}
    rows = group * ROWS
    columns = [pl.ds(c * piece, piece) for c in range(PIECES)]

    for k in range(share):
        for m in range(1, group):
            core_rows[k, m].wait_recv()

        def first(at, k=k):
            cols = pl.ds(at, 256)
            x = arr[k].reshape(rows, width)
            gated = jnp.dot(x, wg[:, cols], preferred_element_type=jnp.float32)
            lifted = jnp.dot(x, wu[:, cols], preferred_element_type=jnp.float32)
            hid[k, :, cols] = (gated / (1.0 + jnp.exp(-gated)) * lifted).astype(jnp.bfloat16)

        tiles(units, 256, first)

    own_w[2].wait()
    for copy in down_copies:
        copy.wait_recv()

    def homeward(k, c):
        cols = columns[c]
        dp_sums[k, c] = go(
            send(
                part.at[k, 0, :, cols], dp_in.at[k, :, cols],
                d_s.at[k, c], d_r.at[k, c], share_peer(back(k, share)),
            )
        )

    def finish(k):
        for m in range(1, group):
            core_sums[k, m].wait_recv()
        for c in range(PIECES):

            def add(at, c=c):
                cols = pl.ds(c * piece + at, 256)
                total = part[k, 0, :, cols].astype(jnp.float32)
                for m in range(1, group):
                    total = total + core_in[k, m, :, cols].astype(jnp.float32)
                part[k, 0, :, cols] = total.astype(jnp.bfloat16)

            tiles(piece, 256, add)
            if relay and k == 3:
                for n, rows_n in enumerate((low, high)):
                    relayed[n, c] = go(
                        send(
                            part.at[3, 0, rows_n, columns[c]], relay_in.at[n, :, columns[c]],
                            r_s.at[n, c], r_r.at[n, c], share_peer(n + 1),
                        )
                    )
            elif k and not relay:
                homeward(k, c)

    order = [3, 1, 2, 0] if relay else [*range(1, share), 0]
    for n, k in enumerate(order):

        def second(at, k=k):
            cols = pl.ds(at, 256)
            made = jnp.dot(hid[k], wd[:, cols], preferred_element_type=jnp.float32)
            part[k, :, :, cols] = made.astype(jnp.bfloat16).reshape(group, ROWS, 256)

        tiles(width, 256, second)
        for m in range(1, group):
            core_sums[k, m] = go(
                send(part.at[k, m], core_in.at[k, m], c_s.at[k, m], c_r.at[k, m], core_peer(group - m))
            )
        if n:
            finish(order[n - 1])

    if relay:
        for c in range(PIECES):
            relayed[0, c].wait_recv()
            relayed[1, c].wait_recv()

            def add_relayed(at, c=c):
                cols = pl.ds(c * piece + at, 256)
                for n, rows_n in enumerate((low, high)):
                    total = part[2 - n, 0, rows_n, cols].astype(jnp.float32)
                    total = total + relay_in[n, :, cols].astype(jnp.float32)
                    part[2 - n, 0, rows_n, cols] = total.astype(jnp.bfloat16)

            tiles(piece, 256, add_relayed)
            homeward(1, c)
            homeward(2, c)
    finish(order[-1])

    home = []
    for c in range(PIECES):
        for k in range(1, share):
            if (k, c) in dp_sums:
                dp_sums[k, c].wait_recv()

        def gather(at, c=c):
            cols = pl.ds(c * piece + at, 256)
            total = part[0, 0, :, cols].astype(jnp.float32)
            for k in range(1, share):
                if (k, c) in dp_sums:
                    total = total + dp_in[k, :, cols].astype(jnp.float32)
            wide[:, cols] = total
            for i in range(EXPERTS):
                full = jnp.concatenate(
                    [wide[i * CAP : (i + 1) * CAP, cols], jnp.zeros((SLOTS - CAP, 256), jnp.float32)]
                )
                to = zout if i else out
                to[i, :, cols] = full.astype(jnp.bfloat16)

        tiles(piece, 256, gather)
        for i in range(1, EXPERTS):
            home.append(
                go(
                    send(
                        zout.at[i, :, columns[c]], out.at[i, :, columns[c]],
                        o_s.at[i, c], o_r.at[i, c], z_peer(EXPERTS - i),
                    )
                )
            )
    for copy in home:
        copy.wait_recv()
    for copy in sent:
        copy.wait_send()


def shared_by(dp, group, width, hidden):
    for share in range(dp, 0, -1):
        if dp % share or hidden % share or hidden // share % 256:
            continue
        block = ROWS * width * 2
        units = hidden // share
        held = (
            block * (share * group * 3 + share + 3)
            + 3 * width * units * 2
            + share * group * ROWS * units * 2
            + 4 * EXPERTS * SLOTS * width * 2
        )
        if held <= VMEM_LIMIT * 7 // 8:
            return share
    return 1


def experts(buffer, gate, up, down):
    dp, group = lax.axis_size("dp"), lax.axis_size("expert") // EXPERTS
    width, hidden = buffer.shape[-1], gate.shape[1]
    share = shared_by(dp, group, width, hidden)
    units = hidden // share
    bf16, dma = jnp.bfloat16, pltpu.SemaphoreType.DMA
    whole = pl.BlockSpec(memory_space=pltpu.VMEM)
    far = pl.BlockSpec(memory_space=pl.ANY)
    pairs = lambda *shape: [dma(shape), dma(shape)]
    return pl.pallas_call(
        functools.partial(kernel, dp, share, group),
        out_shape=jax.ShapeDtypeStruct(buffer.shape, bf16),
        in_specs=[whole, far, far, far],
        out_specs=whole,
        scratch_shapes=[
            pltpu.VMEM((EXPERTS, SLOTS, width), bf16),
            pltpu.VMEM((share, group, ROWS, width), bf16),
            pltpu.VMEM((width, units), bf16),
            pltpu.VMEM((width, units), bf16),
            pltpu.VMEM((units, width), bf16),
            pltpu.VMEM((share, group * ROWS, units), bf16),
            pltpu.VMEM((share, group, ROWS, width), bf16),
            pltpu.VMEM((share, group, ROWS, width), bf16),
            pltpu.VMEM((share, ROWS, width), bf16),
            pltpu.VMEM((2, ROWS // 2, width), bf16),
            pltpu.VMEM((ROWS, width), jnp.float32),
            pltpu.VMEM((EXPERTS, SLOTS, width), bf16),
            *pairs(EXPERTS),
            *pairs(3, dp),
            dma((3,)),
            *pairs(2 * share),
            *pairs(share, group),
            *pairs(share, group),
            *pairs(share, PIECES),
            *pairs(2, PIECES),
            *pairs(EXPERTS, PIECES),
            dma((1,)),
        ],
        compiler_params=pltpu.CompilerParams(
            collective_id=0, has_side_effects=True, vmem_limit_bytes=VMEM_LIMIT
        ),
        cost_estimate=pl.CostEstimate(
            flops=6 * share * group * ROWS * width * units,
            bytes_accessed=3 * width * hidden * 2,
            transcendentals=share * group * ROWS * units,
        ),
    )(buffer, gate, up, down)


def body(
    tokens, modality, local_expert, combine_weight, norm_gain, gate_weight, up_weight, down_weight
):
    count, width = tokens.shape
    resid = tokens.astype(jnp.float32)
    root_mean = jnp.sqrt(jnp.mean(resid * resid, axis=1, keepdims=True) + 1e-05)
    row_gain = jnp.where(modality[:, None] == 0, norm_gain[0][None, :], norm_gain[1][None, :])
    normed = (resid / root_mean * row_gain).astype(jnp.bfloat16)
    route = modality * EXP_MOD + local_expert
    at = jnp.arange(count, dtype=jnp.int32)
    earlier = (route[:, None] == route[None, :]) & (at[None, :] < at[:, None])
    row_rank = jnp.sum(earlier.astype(jnp.int32), axis=1)
    own = lax.axis_index("expert") // (lax.axis_size("expert") // EXPERTS)
    position = (route - own + EXPERTS) % EXPERTS * SLOTS + row_rank
    placing = (
        position[:, None] == jnp.arange(EXPERTS * SLOTS, dtype=jnp.int32)[None, :]
    ).astype(jnp.bfloat16)
    buffer = jnp.einsum("ts,td->sd", placing, normed, preferred_element_type=jnp.float32)
    buffer = buffer.astype(jnp.bfloat16).reshape(EXPERTS, SLOTS, width)
    summed = experts(buffer, gate_weight, up_weight, down_weight)
    moe_out = jnp.dot(
        placing, summed.reshape(EXPERTS * SLOTS, width), preferred_element_type=jnp.float32
    )
    return (resid + combine_weight[:, None] * moe_out).astype(jnp.bfloat16)


def solution(mesh):
    in_specs = (
        P(("dp", "expert"), None),
        P(("dp", "expert")),
        P(("dp", "expert")),
        P(("dp", "expert")),
        P(),
        P("dp", "expert"),
        P("dp", "expert"),
        P("expert", "dp"),
    )
    out_specs = P(("dp", "expert"), None)
    return jax.shard_map(body, mesh=mesh, in_specs=in_specs, out_specs=out_specs, check_vma=False)
```
